512 devices in a mesh: ctx: 64 (over x, z), tp: 8 (over y, core).
Axes of the slice: x: 4, y: 4, z: 16, core: 2. Of those that a mesh axis runs over, the one named last changes fastest.
Arguments:
- query_in: bfloat16 [16384, 4096], P('ctx', 'tp'), may hold values from -6 to 6
- key_in: bfloat16 [16384, 4096], P('ctx', 'tp'), may hold values from -6 to 6
- value_in: bfloat16 [16384, 4096], P('ctx', 'tp'), may hold values from -6 to 6
- short_weights: float32 [3, 3, 4096], P(None, None, 'tp'), may hold values from -3 to 3
- long_filter: float32 [4096, 16384], P(('tp', 'ctx')), may hold values from -1.6 to 1.6
- skip_gain: float32 [4096], P(('tp', 'ctx')), may hold values from -4 to 4
- cotangent: bfloat16 [16384, 4096], P('ctx', 'tp'), may hold values from -10.8 to 10.8
Outputs:
- mixed_out: bfloat16 [16384, 4096], P('ctx', 'tp')
- d_query: bfloat16 [16384, 4096], P('ctx', 'tp')
- d_key: bfloat16 [16384, 4096], P('ctx', 'tp')
- d_value: bfloat16 [16384, 4096], P('ctx', 'tp')
- d_filter: float32 [4096, 16384], P(('tp', 'ctx'))
- d_skip: float32 [4096], P(('tp', 'ctx'))
- d_short: float32 [3, 3, 4096], P(None, None, 'tp')
The draws below stay inside these ranges and needn't reach their ends.
All inputs are finite; a program needn't handle non-finite values.
Results may differ from the reference program's by a relative error of at most 0.0064.
Values may be sent and summed in bfloat16 or wider, within the bound.
No kernel may reach another device: no remote copies, remote signals or barrier semaphores. Data moves between devices by JAX's collectives and lax.ppermute only.
A program may use at most 64 MiB of HBM per device.

```python
import math
import jax
import jax.numpy as jnp
from jax import lax

D = 4096
TAPS = 3
L = 16384


def draw_long_filter(key, part):
    key = jax.random.fold_in(key, 7)
    keys = jax.random.split(key, 6)
    share = 0.5
    noise = jnp.clip(jax.random.normal(keys[5], (D, L), jnp.float32), -6.0, 6.0)
    pick = jax.random.uniform(keys[0], (D, 1), jnp.float32)
    slow_rate = jax.random.uniform(keys[1], (D, 1), jnp.float32, 0.05 / L, 0.5 / L)
    fast_rate = jnp.exp(jax.random.uniform(keys[2], (D, 1), jnp.float32, math.log(1.0 / 50.0), math.log(1.0 / 30.0)))
    rate = jnp.where(pick < share, slow_rate, fast_rate)
    spots = jax.random.randint(keys[3], (D, 2), 1, L)
    drops = jax.random.uniform(keys[4], (D, 2), jnp.float32, 0.2, 0.5)
    lags = jnp.arange(L, dtype=jnp.int32)
    first_hit = (lags[None, :] >= spots[:, 0:1]).astype(jnp.float32)
    second_hit = (lags[None, :] >= spots[:, 1:2]).astype(jnp.float32)
    envelope = jnp.exp(-rate * lags[None, :].astype(jnp.float32))
    envelope = envelope * (1.0 - drops[:, 0:1] * first_hit) * (1.0 - drops[:, 1:2] * second_hit)
    energy = jnp.expm1(-2.0 * rate * L) / jnp.expm1(-2.0 * rate)
    return (noise * envelope / jnp.sqrt(energy)).astype(jnp.float32)


def draw_cotangent(key, part):
    key = jax.random.fold_in(key, 11)
    lags = jnp.arange(L, dtype=jnp.int32)[:, None].astype(jnp.float32)
    ramp_line = 0.6 + 1.2 * lags / L
    noise = jnp.clip(jax.random.normal(key, (L, D), jnp.float32), -6.0, 6.0)
    return (noise * ramp_line).astype(jnp.bfloat16)


def block_scale(key, extent, cuts, least, high):
    factor_of, own = 1.0, jax.random.fold_in(key, 6)
    for position, shards_of in cuts:
        steps = jnp.exp(jax.random.uniform(jax.random.fold_in(own, position), (shards_of,), jnp.float32, least / len(cuts), high / len(cuts)))
        factor_of = factor_of * jnp.repeat(steps, extent[position] // shards_of).reshape([-1 if axis == position else 1 for axis in range(len(extent))])
    return factor_of


def centred(rng, extent, spread, limit, cuts=(), kind=jnp.bfloat16):
    values = jax.random.normal(rng, extent, jnp.float32) * spread
    if len(cuts) > 0:
        values = block_scale(rng, extent, cuts, -0.22, 0.18) * values
    return jnp.clip(values, min=-limit, max=limit).astype(kind)


def setup_inputs(seed: int = 0) -> dict:
    key_list = jax.random.split(jax.random.key(seed), 8)
    query_in = centred(key_list[0], (L, D), 1.0, 6.0, ((0, 64), (1, 8)))
    key_in = centred(key_list[1], (L, D), 1.0, 6.0, ((0, 64), (1, 8)))
    value_in = centred(key_list[2], (L, D), 1.0, 6.0, ((0, 64), (1, 8)))
    short_weights = centred(key_list[3], (3, TAPS, D), 0.6, 3.0, ((2, 8),), jnp.float32)
    long_filter = draw_long_filter(jax.random.fold_in(key_list[7], 71), 0)
    skip_gain = centred(key_list[5], (D,), 1.0, 4.0, ((0, 512),), jnp.float32)
    cotangent = draw_cotangent(jax.random.fold_in(key_list[7], 71), 0)
    return {"query_in": query_in, "key_in": key_in, "value_in": value_in, "short_weights": short_weights, "long_filter": long_filter, "skip_gain": skip_gain, "cotangent": cotangent}


def short_conv(signal, weights):
    padded = jnp.pad(signal, ((2, 0), (0, 0)))
    return weights[0] * padded[2:] + weights[1] * padded[1:-1] + weights[2] * padded[:-2]


def short_back(grads, weights):
    padded = jnp.pad(grads, ((0, 2), (0, 0)))
    return weights[0] * padded[:-2] + weights[1] * padded[1:-1] + weights[2] * padded[2:]


def tap_grads(grads, signal):
    padded = jnp.pad(signal, ((2, 0), (0, 0)))
    rows = grads.shape[0]
    return jnp.stack([jnp.sum(grads * padded[2 - offset:2 - offset + rows], axis=0) for offset in range(3)])


def reference(query_in, key_in, value_in, short_weights, long_filter, skip_gain, cotangent):
    query_f = query_in.astype(jnp.float32)
    key_f = key_in.astype(jnp.float32)
    value_f = value_in.astype(jnp.float32)
    conv_query = lax.optimization_barrier(short_conv(query_f, short_weights[0]).astype(jnp.bfloat16))
    conv_key = short_conv(key_f, short_weights[1])
    conv_value = short_conv(value_f, short_weights[2])
    gated_in = (conv_key * conv_value).astype(jnp.bfloat16)
    query_cf = conv_query.astype(jnp.float32)
    cot_f = cotangent.astype(jnp.float32)
    d_inner = (cot_f * query_cf).astype(jnp.bfloat16)
    block_cols = 256
    block_count = D // block_cols
    grad_scale = 1.0 / (L ** 0.5)

    def to_blocks(array):
        return array.T.reshape(block_count, block_cols, L)

    def from_blocks(array):
        return array.reshape(D, L).T

    def channel_block(pieces):
        gated_b, dinner_b, filter_b, skip_b = pieces
        gated_f = gated_b.astype(jnp.float32)
        dinner_f = dinner_b.astype(jnp.float32)
        total_len = 2 * L
        spec_gated = jnp.fft.rfft(gated_f, n=total_len, axis=1)
        spec_filter = jnp.fft.rfft(filter_b, n=total_len, axis=1)
        long_part = jnp.fft.irfft(spec_gated * spec_filter, n=total_len, axis=1)[:, :L]
        inner_b = (long_part + skip_b[:, None] * gated_f).astype(jnp.bfloat16)
        spec_grad = jnp.fft.rfft(dinner_f, n=total_len, axis=1)
        corr_filter = jnp.fft.irfft(jnp.conj(spec_filter) * spec_grad, n=total_len, axis=1)[:, :L]
        dgated_b = (corr_filter + skip_b[:, None] * dinner_f).astype(jnp.bfloat16)
        dfilter_b = jnp.fft.irfft(jnp.conj(spec_gated) * spec_grad, n=total_len, axis=1)[:, :L] * grad_scale
        dskip_b = jnp.sum(dinner_f * gated_f, axis=1) * grad_scale
        return inner_b, dgated_b, dfilter_b, dskip_b

    results = lax.map(channel_block, (to_blocks(gated_in), to_blocks(d_inner),
                                      long_filter.reshape(block_count, block_cols, L),
                                      skip_gain.reshape(block_count, block_cols)))
    inner_sum = from_blocks(results[0]).astype(jnp.float32)
    d_gated = from_blocks(results[1]).astype(jnp.float32)
    d_filter = results[2].reshape(D, L)
    d_skip = results[3].reshape(D)
    mixed_out = (query_cf * inner_sum).astype(jnp.bfloat16)
    dconv_query = lax.optimization_barrier((cot_f * inner_sum).astype(jnp.bfloat16)).astype(jnp.float32)
    dconv_key = d_gated * conv_value
    dconv_value = d_gated * conv_key
    d_query = short_back(dconv_query, short_weights[0]).astype(jnp.bfloat16)
    d_key = short_back(dconv_key, short_weights[1]).astype(jnp.bfloat16)
    d_value = short_back(dconv_value, short_weights[2]).astype(jnp.bfloat16)
    d_short = jnp.stack([tap_grads(dconv_query, query_f), tap_grads(dconv_key, key_f),
                         tap_grads(dconv_value, value_f)]) * grad_scale
    return mixed_out, d_query, d_key, d_value, d_filter, d_skip, d_short
```

```python
import jax
import jax.numpy as jnp
import ml_dtypes
import numpy as np
from jax import lax
from jax.experimental import pallas as pl
from jax.experimental.pallas import tpu as pltpu
from jax.sharding import PartitionSpec as P

ROWS = 128
COLS = 128
LANES = 128
OWN = 8
F32 = jnp.float32
BF16 = jnp.bfloat16
VMEM = pltpu.VMEM


def halves(table):
    high = table.astype(np.float32).astype(ml_dtypes.bfloat16)
    low = (table - high.astype(np.float64)).astype(np.float32).astype(ml_dtypes.bfloat16)
    return high, low


def tables():
    r = np.arange(128, dtype=np.int64)
    full = 4 * ROWS * COLS
    first = 2.0 * np.pi / 512 * ((r[None, :] * (2 * r[:, None] + 1)) % 512)
    turn = -2.0 * np.pi / full * ((r[None, :] * (2 * r[:, None] + 1)) % full)
    last = 2.0 * np.pi / 128 * ((r[:, None] * r[None, :]) % 128)
    w_high, w_low = halves(np.concatenate([np.cos(first), -np.sin(first)], 0))
    t = np.block([[np.cos(last), -np.sin(last)], [np.sin(last), np.cos(last)]])
    t_high, t_low = halves(t)
    i_high, i_low = halves(t.T.copy())
    back = np.concatenate([np.cos(first).T, -np.sin(first).T], 1) * (2.0 / (2 * ROWS * COLS))
    b_high, b_low = halves(back)
    return dict(
        first_pair=np.concatenate([w_high, w_low], 1),
        first_three=np.concatenate([w_high, w_low, w_high], 1),
        turn_re=np.cos(turn).astype(np.float32),
        turn_im=np.sin(turn).astype(np.float32),
        last=np.concatenate([t_high, t_high, t_low], 0),
        last_back=np.concatenate([i_high, i_high, i_low], 0),
        first_back=np.concatenate([b_high, b_low, b_high], 1),
    )


def dot(a, b):
    return jnp.dot(a, b, preferred_element_type=F32)


def split(x):
    high = x.astype(BF16)
    return high, (x - high.astype(F32)).astype(BF16)


def rounded(x):
    return x.astype(BF16).astype(F32)


def wide(x):
    high, low = split(x)
    return jnp.concatenate([high, low, high], axis=1)


def tall(x):
    high, low = split(x)
    return jnp.concatenate([high, high, low], axis=0)


def turned(part, tr, ti):
    re, im = part[:128], part[128:]
    return jnp.concatenate([re * tr - im * ti, re * ti + im * tr], axis=1)


def turned_back(part, tr, ti):
    re, im = part[:, :128], part[:, 128:]
    return jnp.concatenate([re * tr + im * ti, im * tr - re * ti], axis=0)


def pack_kernel(q, k, v, c, out):
    for j in range(4):
        cols = slice(128 * j, 128 * j + 128)
        for top, low, off in ((k, q, 0), (v, c, 256)):
            upper = top[:, cols].astype(F32).T.reshape(16, OWN, 256)
            lower = low[:, cols].astype(F32).T.reshape(16, OWN, 256)
            both = jnp.concatenate([upper, lower], axis=1)
            out[16 * j : 16 * j + 16, :, off : off + 256] = both.astype(BF16)


def filter_kernel(f, first, tr, ti, last, out, rows):
    for a in range(ROWS):
        rows[8 * a : 8 * a + 8, :] = f[:, 128 * a : 128 * a + 128]
    for p in range(OWN // 2):
        x = jnp.concatenate(
            [rows[pl.ds(2 * p + i, ROWS, stride=OWN), :] for i in range(2)], axis=1
        )
        part = dot(first[...], tall(x))
        lhs = jnp.concatenate(
            [turned(part[:, 128 * i : 128 * i + 128], tr[...], ti[...]) for i in range(2)], axis=0
        )
        spec = dot(wide(lhs), last[...])
        out[2 * p] = spec[:128]
        out[2 * p + 1] = spec[128:]


def lagged(x, lane, by):
    r = pltpu.roll(x, by, axis=2)
    return jnp.where(lane < by, r[1:9], r[2:10])


def channel_kernel(
    x, w, skip, filt, first, tr, ti, last, last_back, first_back,
    out, cross, dskip,
    gated_s, grad_s, inner_s, corr_s, cot_s, conv_s, raw_s,
):
    lane = lax.broadcasted_iota(jnp.int32, (8, OWN, LANES), 2)
    scale = 1.0 / 128.0

    def blocks(value, upper, off):
        rows = slice(0, 8) if upper else slice(8, 16)
        lo = value[:, rows, off : off + 128]
        hi = value[:, rows, off + 128 : off + 256]
        return jnp.stack([lo, hi], axis=1).reshape(-1, OWN, LANES)

    def convolve(i, carry):
        s0 = 4 * i
        keep = jnp.where(i > 0, 1.0, 0.0).astype(F32)
        before = x[pl.ds(jnp.maximum(s0 - 1, 0), 1)].astype(F32) * keep
        here = x[pl.ds(s0, 4)].astype(F32)
        value = jnp.concatenate([before, here], axis=0)
        at = pl.ds(8 * i, 8)
        convs = []
        for s, (upper, off) in enumerate(((False, 0), (True, 0), (True, 256))):
            seq = blocks(value, upper, off)
            lags = [seq[2:], lagged(seq, lane, 1), lagged(seq, lane, 2)]
            for j in range(3):
                raw_s[3 * s + j, at] = lags[j]
            convs.append(
                w[3 * s] * lags[0] + w[3 * s + 1] * lags[1] + w[3 * s + 2] * lags[2]
            )
        cot = blocks(here, False, 256)
        cot_s[at] = cot
        conv_s[0, at] = convs[1]
        conv_s[1, at] = convs[2]
        flat = pl.ds(64 * i, 64)
        gated_s[flat, :] = rounded(convs[1] * convs[2]).reshape(64, LANES)
        grad_s[flat, :] = rounded(cot * rounded(convs[0])).reshape(64, LANES)
        return carry

    lax.fori_loop(0, 16, convolve, 0)

    for ch in range(OWN):
        own = pl.ds(ch, ROWS, stride=OWN)
        pair = jnp.concatenate([gated_s[own, :], grad_s[own, :]], axis=1).astype(BF16)
        part = dot(first[...], jnp.concatenate([pair, pair], axis=0))
        lhs = jnp.concatenate(
            [turned(part[:, 128 * i : 128 * i + 128], tr[...], ti[...]) for i in range(2)], axis=0
        )
        spec = dot(wide(lhs), last[...])
        gr, gi = spec[:128, :128], spec[:128, 128:]
        dr, di = spec[128:, :128], spec[128:, 128:]
        fr, fi = filt[ch][:, :128], filt[ch][:, 128:]
        cross[ch] = jnp.concatenate([gr * dr + gi * di, gr * di - gi * dr], axis=1)
        inner = jnp.concatenate([gr * fr - gi * fi, gr * fi + gi * fr], axis=1)
        corr = jnp.concatenate([fr * dr + fi * di, fr * di - fi * dr], axis=1)
        back = dot(wide(jnp.concatenate([inner, corr], axis=0)), last_back[...])
        turn = jnp.concatenate(
            [turned_back(back[128 * i : 128 * i + 128], tr[...], ti[...]) for i in range(2)], axis=1
        )
        y = dot(first_back[...], tall(turn))
        inner_s[own, :] = y[:, :128]
        corr_s[own, :] = y[:, 128:]

    def finish(i, sums):
        at = pl.ds(8 * i, 8)
        flat = pl.ds(64 * i, 64)
        gated = gated_s[flat, :].reshape(8, OWN, LANES)
        grad = grad_s[flat, :].reshape(8, OWN, LANES)
        inner = rounded(inner_s[flat, :].reshape(8, OWN, LANES) + skip[...] * gated)
        dgated = rounded(corr_s[flat, :].reshape(8, OWN, LANES) + skip[...] * grad)
        dconv = (rounded(cot_s[at] * inner), dgated * conv_s[1, at], dgated * conv_s[0, at])
        terms = [dconv[s] * raw_s[3 * s + j, at] for s in range(3) for j in range(3)]
        terms.append(grad * gated)
        sums = tuple(total + jnp.sum(term, axis=0) for total, term in zip(sums, terms))
        for value, off in ((dgated, 0), (inner, 256)):
            value = value.reshape(4, 2, OWN, LANES)
            both = jnp.concatenate([value[:, 0], value[:, 1]], axis=2)
            out[pl.ds(4 * i, 4), :, off : off + 256] = both.astype(BF16)
        return sums

    zero = jnp.zeros((OWN, LANES), F32)
    sums = lax.fori_loop(0, 16, finish, (zero,) * 10)
    totals = [jnp.sum(total, axis=1, keepdims=True) * scale for total in sums]
    dskip[...] = jnp.broadcast_to(totals[9], (OWN, LANES))

    spot = lax.broadcasted_iota(jnp.int32, (OWN, LANES), 1)
    shared = zero
    for n in range(9):
        value = jnp.broadcast_to(totals[n], (OWN, LANES))
        high = rounded(value)
        mid = rounded(value - high)
        for base, piece in ((0, high), (16, mid), (32, value - high - mid)):
            shared = jnp.where(spot == base + n, piece, shared)
    for g in range(4):
        s0 = 16 * g
        edge = []
        for off, by in ((0, 48), (256, 50)):
            if g < 3:
                after = out[s0 : s0 + 32, :, off : off + 128].astype(F32)[1:17]
            else:
                after = out[s0 : s0 + 16, :, off : off + 128].astype(F32)
                after = jnp.concatenate([after[1:], jnp.zeros((1, OWN, LANES), F32)], axis=0)
            edge.append(pltpu.roll(after, by, axis=2))
        rest = jnp.where(spot < 50, edge[0], edge[1])
        extra = jnp.where(spot < 48, shared, jnp.where(spot < 52, rest, 0.0))
        out[s0 : s0 + 16, :, 512:640] = extra.astype(BF16)


def cross_kernel(cross, tr, ti, last_back, first_back, out, rows):
    for p in range(OWN // 2):
        both = jnp.concatenate([cross[2 * p], cross[2 * p + 1]], axis=0)
        back = dot(wide(both), last_back[...])
        turn = jnp.concatenate(
            [turned_back(back[128 * i : 128 * i + 128], tr[...], ti[...]) for i in range(2)], axis=1
        )
        y = dot(first_back[...], tall(turn)) * (1.0 / 128.0)
        for i in range(2):
            rows[pl.ds(2 * p + i, ROWS, stride=OWN), :] = y[:, 128 * i : 128 * i + 128]
    for a in range(ROWS):
        out[:, 128 * a : 128 * a + 128] = rows[8 * a : 8 * a + 8, :]


def token_kernel(got, q, k, v, c, prev, nxt, w, mixed, dq, dk, dv, dshort):
    for j in range(4):
        cols = slice(128 * j, 128 * j + 128)
        own = slice(16 * j, 16 * j + 16)

        def columns(off, width):
            return got[own, :, off : off + width].astype(F32).reshape(128, width).T

        dgated = columns(0, 256)
        inner = columns(256, 256)
        extra = columns(512, 128)
        for s in range(3):
            for n in range(3):
                at = 3 * s + n
                total = extra[at : at + 1] + extra[16 + at : 17 + at] + extra[32 + at : 33 + at]
                dshort[s, n : n + 1, cols] = total
        weight = [[w[s, n : n + 1, cols] for n in range(3)] for s in range(3)]
        cot = c[:, cols].astype(F32)
        cot_n = nxt[4:6, cols]

        def conv(seq, s):
            rows = seq.shape[0] - 2
            return (
                weight[s][0] * seq[2:] + weight[s][1] * seq[1 : 1 + rows] + weight[s][2] * seq[:rows]
            )

        def back(seq, s):
            total = (
                weight[s][0] * seq[:256] + weight[s][1] * seq[1:257] + weight[s][2] * seq[2:258]
            )
            return total.astype(BF16)

        q_ext = jnp.concatenate([prev[0:2, cols], q[:, cols].astype(F32)], axis=0)
        query = rounded(conv(q_ext, 0))
        mixed[:, cols] = (query * inner).astype(BF16)
        dconv = jnp.concatenate([rounded(cot * inner), rounded(cot_n * extra[50:52])], axis=0)
        dq[:, cols] = back(dconv, 0)
        dgated_ext = jnp.concatenate([dgated, extra[48:50]], axis=0)
        k_ext = jnp.concatenate([prev[2:4, cols], k[:, cols].astype(F32), nxt[0:2, cols]], axis=0)
        v_ext = jnp.concatenate([prev[4:6, cols], v[:, cols].astype(F32), nxt[2:4, cols]], axis=0)
        dk[:, cols] = back(dgated_ext * conv(v_ext, 2), 1)
        dv[:, cols] = back(dgated_ext * conv(k_ext, 1), 2)


def call(kernel, outs, scratch=(), flops=0, moved=0, limit=24):
    one = not isinstance(outs, list)
    shapes = [outs] if one else outs
    return pl.pallas_call(
        kernel,
        out_shape=shapes[0] if one else shapes,
        scratch_shapes=list(scratch),
        compiler_params=pltpu.CompilerParams(vmem_limit_bytes=limit << 20),
        cost_estimate=pl.CostEstimate(flops=flops, bytes_accessed=moved, transcendentals=0),
    )


def shape(*dims, kind=F32):
    return jax.ShapeDtypeStruct(dims, kind)


def body(query_in, key_in, value_in, short_weights, long_filter, skip_gain, cotangent):
    t = tables()
    turns = (t["turn_re"], t["turn_im"])
    count = lax.axis_size("ctx")
    here = lax.axis_index("ctx")

    packed = call(pack_kernel, shape(64, 16, 512, kind=BF16), moved=2 << 20)(
        query_in, key_in, value_in, cotangent
    )
    seqs = lax.all_to_all(packed, "ctx", split_axis=0, concat_axis=0, tiled=True)

    spectrum = call(
        filter_kernel, shape(OWN, 128, 256), [VMEM((1024, LANES), F32)],
        flops=10**9, moved=2 << 20,
    )(long_filter, t["first_three"], *turns, t["last"])

    ends = jnp.concatenate([query_in[254:], key_in[254:], value_in[254:]], axis=0)
    starts = jnp.concatenate([key_in[:2], value_in[:2], cotangent[:2]], axis=0)
    prev = lax.ppermute(ends, "ctx", [(i, i + 1) for i in range(count - 1)]).astype(F32)
    nxt = lax.ppermute(starts, "ctx", [(i + 1, i) for i in range(count - 1)]).astype(F32)

    own_w = lax.dynamic_slice_in_dim(short_weights, OWN * here, OWN, axis=2).reshape(9, OWN, 1)
    own_w = jnp.broadcast_to(own_w, (9, OWN, LANES))
    own_skip = jnp.broadcast_to(skip_gain[:, None], (OWN, LANES))

    big = VMEM((128, OWN, LANES), F32)
    flat = VMEM((1024, LANES), F32)
    answer, cross, dskip = call(
        channel_kernel,
        [shape(64, OWN, 640, kind=BF16), shape(OWN, 128, 256), shape(OWN, LANES)],
        [flat, flat, flat, flat, big, VMEM((2, 128, OWN, LANES), F32), VMEM((9, 128, OWN, LANES), F32)],
        flops=4 * 10**9, moved=4 << 20,
    )(seqs, own_w, own_skip, spectrum, t["first_pair"], *turns, t["last"], t["last_back"], t["first_back"])

    got = lax.all_to_all(answer, "ctx", split_axis=0, concat_axis=0, tiled=True)

    d_filter = call(
        cross_kernel, shape(OWN, 16384), [flat], flops=10**9, moved=2 << 20
    )(cross, *turns, t["last_back"], t["first_back"])

    tokens = shape(256, 512, kind=BF16)
    mixed, d_query, d_key, d_value, d_short = call(
        token_kernel, [tokens, tokens, tokens, tokens, shape(3, 3, 512)], moved=3 << 20
    )(got, query_in, key_in, value_in, cotangent, prev, nxt, short_weights)
    return (mixed, d_query, d_key, d_value, d_filter, dskip[:, 0], d_short)


def solution(mesh):
    tokens = P("ctx", "tp")
    rows = P(("tp", "ctx"), None)
    taps = P(None, None, "tp")
    flat = P(("tp", "ctx"))
    in_specs = (tokens, tokens, tokens, taps, rows, flat, tokens)
    out_specs = (tokens, tokens, tokens, tokens, rows, flat, taps)
    return jax.shard_map(body, mesh=mesh, in_specs=in_specs, out_specs=out_specs, check_vma=False)
```

```python
import jax
import jax.numpy as jnp
import ml_dtypes
import numpy as np
from jax import lax
from jax.experimental import pallas as pl
from jax.experimental.pallas import tpu as pltpu
from jax.sharding import PartitionSpec as P

ROWS = 128
COLS = 128
LANES = 128
OWN = 8
F32 = jnp.float32
BF16 = jnp.bfloat16
VMEM = pltpu.VMEM
HBM = pl.BlockSpec(memory_space=pltpu.HBM)
WHOLE = pl.BlockSpec(memory_space=pltpu.VMEM)
GROUP = 4
SPARE = 24
TAIL = 2048


def halves(table):
    high = table.astype(np.float32).astype(ml_dtypes.bfloat16)
    low = (table - high.astype(np.float64)).astype(np.float32).astype(ml_dtypes.bfloat16)
    return high, low


def tables():
    r = np.arange(128, dtype=np.int64)
    full = 4 * ROWS * COLS
    first = 2.0 * np.pi / 512 * ((r[None, :] * (2 * r[:, None] + 1)) % 512)
    turn = -2.0 * np.pi / full * ((r[None, :] * (2 * r[:, None] + 1)) % full)
    last = 2.0 * np.pi / 128 * ((r[:, None] * r[None, :]) % 128)
    w_high, w_low = halves(np.concatenate([np.cos(first), -np.sin(first)], 0))
    t = np.block([[np.cos(last), -np.sin(last)], [np.sin(last), np.cos(last)]])
    t_high, t_low = halves(t)
    i_high, i_low = halves(t.T.copy())
    back = np.concatenate([np.cos(first).T, -np.sin(first).T], 1) * (2.0 / (2 * ROWS * COLS))
    b_high, b_low = halves(back)
    return dict(
        first_pair=np.concatenate([w_high, w_low], 1),
        first_three=np.concatenate([w_high, w_low, w_high], 1),
        turn_re=np.cos(turn).astype(np.float32),
        turn_im=np.sin(turn).astype(np.float32),
        last=np.concatenate([t_high, t_high, t_low], 0),
        last_back=np.concatenate([i_high, i_high, i_low], 0),
        first_back=np.concatenate([b_high, b_low, b_high], 1),
    )


def dot(a, b):
    return jnp.dot(a, b, preferred_element_type=F32)


def split(x):
    high = x.astype(BF16)
    return high, (x - high.astype(F32)).astype(BF16)


def rounded(x):
    return x.astype(BF16).astype(F32)


def wide(x):
    high, low = split(x)
    return jnp.concatenate([high, low, high], axis=1)


def tall(x):
    high, low = split(x)
    return jnp.concatenate([high, high, low], axis=0)


def turned(part, tr, ti):
    re, im = part[:128], part[128:]
    return jnp.concatenate([re * tr - im * ti, re * ti + im * tr], axis=1)


def turned_back(part, tr, ti):
    re, im = part[:, :128], part[:, 128:]
    return jnp.concatenate([re * tr + im * ti, im * tr - re * ti], axis=0)


def copy(source, target, sem):
    return pltpu.make_async_copy(source, target, sem)


def pack_kernel(q, k, v, c, out, q_v, k_v, v_v, c_v, out_v, sems):
    loads = [copy(a, b, sems.at[i]) for i, (a, b) in enumerate(((k, k_v), (q, q_v), (v, v_v), (c, c_v)))]
    for load in loads:
        load.start()
    stores = []
    for load in loads:
        load.wait()
    for j in range(4):
        cols = slice(128 * j, 128 * j + 128)
        for top, low, off in ((k_v, q_v, 0), (v_v, c_v, 256)):
            upper = top[:, cols].astype(F32).T.reshape(16, OWN, 256)
            lower = low[:, cols].astype(F32).T.reshape(16, OWN, 256)
            both = jnp.concatenate([upper, lower], axis=1)
            out_v[16 * j : 16 * j + 16, :, off : off + 256] = both.astype(BF16)
        part = pl.ds(16 * j, 16)
        stores.append(copy(out_v.at[part], out.at[part], sems.at[4 + j]))
        stores[j].start()
    for store in stores:
        store.wait()


def filter_kernel(here, f, w, skip, first, tr, ti, last, out, own_w, rows):
    wanted = OWN * here[0] + lax.broadcasted_iota(jnp.int32, (OWN, 512), 0)
    mine = lax.broadcasted_iota(jnp.int32, (OWN, 512), 1) == wanted
    for s in range(3):
        for n in range(3):
            value = jnp.sum(jnp.where(mine, w[s, n : n + 1, :], 0.0), axis=1, keepdims=True)
            own_w[3 * s + n] = jnp.broadcast_to(value, (OWN, LANES))
    own_w[9] = jnp.broadcast_to(skip[...], (OWN, LANES))
    for a in range(ROWS):
        rows[8 * a : 8 * a + 8, :] = f[:, 128 * a : 128 * a + 128]
    for p in range(OWN // 2):
        x = jnp.concatenate(
            [rows[pl.ds(2 * p + i, ROWS, stride=OWN), :] for i in range(2)], axis=1
        )
        part = dot(first[...], tall(x))
        lhs = jnp.concatenate(
            [turned(part[:, 128 * i : 128 * i + 128], tr[...], ti[...]) for i in range(2)], axis=0
        )
        spec = dot(wide(lhs), last[...])
        out[2 * p] = spec[:128]
        out[2 * p + 1] = spec[128:]


def lagged(x, lane, by):
    r = pltpu.roll(x, by, axis=2)
    return jnp.where(lane < by, r[1:9], r[2:10])


def channel_kernel(
    x, w, filt, first, tr, ti, last, last_back, first_back,
    out, cross, dskip,
    gated_s, grad_s, inner_s, corr_s, cot_s, conv_s, raw_s, edge_s, filt_v, cross_v, out_v, sems,
):
    load = copy(filt.at[pl.ds(0, OWN)], filt_v, sems.at[0])
    load.start()
    lane = lax.broadcasted_iota(jnp.int32, (8, OWN, LANES), 2)
    scale = 1.0 / 128.0

    def blocks(value, upper, off):
        rows = slice(0, 8) if upper else slice(8, 16)
        lo = value[:, rows, off : off + 128]
        hi = value[:, rows, off + 128 : off + 256]
        return jnp.stack([lo, hi], axis=1).reshape(-1, OWN, LANES)

    def convolve(i, carry):
        s0 = 4 * i
        keep = jnp.where(i > 0, 1.0, 0.0).astype(F32)
        before = x[pl.ds(jnp.maximum(s0 - 1, 0), 1)].astype(F32) * keep
        here = x[pl.ds(s0, 4)].astype(F32)
        value = jnp.concatenate([before, here], axis=0)
        at = pl.ds(8 * i, 8)
        convs = []
        for s, (upper, off) in enumerate(((False, 0), (True, 0), (True, 256))):
            seq = blocks(value, upper, off)
            lags = [seq[2:], lagged(seq, lane, 1), lagged(seq, lane, 2)]
            for j in range(3):
                raw_s[3 * s + j, at] = lags[j]
            convs.append(
                w[3 * s] * lags[0] + w[3 * s + 1] * lags[1] + w[3 * s + 2] * lags[2]
            )
        cot = blocks(here, False, 256)
        cot_s[at] = cot
        conv_s[0, at] = convs[1]
        conv_s[1, at] = convs[2]
        flat = pl.ds(64 * i, 64)
        gated_s[flat, :] = rounded(convs[1] * convs[2]).reshape(64, LANES)
        grad_s[flat, :] = rounded(cot * rounded(convs[0])).reshape(64, LANES)
        return carry

    lax.fori_loop(0, 16, convolve, 0)

    load.wait()
    stores = []
    for g in range(OWN // GROUP):
        chans = range(GROUP * g, GROUP * g + GROUP)
        lhs = []
        for ch in chans:
            own = pl.ds(ch, ROWS, stride=OWN)
            pair = jnp.concatenate([gated_s[own, :], grad_s[own, :]], axis=1).astype(BF16)
            part = dot(first[...], jnp.concatenate([pair, pair], axis=0))
            lhs += [turned(part[:, 128 * i : 128 * i + 128], tr[...], ti[...]) for i in range(2)]
        specs = dot(wide(jnp.concatenate(lhs, axis=0)), last[...])
        lhs = []
        for n, ch in enumerate(chans):
            spec = specs[256 * n : 256 * n + 256]
            gr, gi = spec[:128, :128], spec[:128, 128:]
            dr, di = spec[128:, :128], spec[128:, 128:]
            fr, fi = filt_v[ch][:, :128], filt_v[ch][:, 128:]
            cross_v[ch] = jnp.concatenate([gr * dr + gi * di, gr * di - gi * dr], axis=1)
            lhs.append(jnp.concatenate([gr * fr - gi * fi, gr * fi + gi * fr], axis=1))
            lhs.append(jnp.concatenate([fr * dr + fi * di, fr * di - fi * dr], axis=1))
        backs = dot(wide(jnp.concatenate(lhs, axis=0)), last_back[...])
        for n, ch in enumerate(chans):
            own = pl.ds(ch, ROWS, stride=OWN)
            back = backs[256 * n : 256 * n + 256]
            turn = jnp.concatenate(
                [turned_back(back[128 * i : 128 * i + 128], tr[...], ti[...]) for i in range(2)], axis=1
            )
            y = dot(first_back[...], tall(turn))
            inner_s[own, :] = y[:, :128]
            corr_s[own, :] = y[:, 128:]
        part = pl.ds(GROUP * g, GROUP)
        stores.append(copy(cross_v.at[part], cross.at[part], sems.at[1 + g]))
        stores[g].start()

    def finish(i, sums):
        at = pl.ds(8 * i, 8)
        flat = pl.ds(64 * i, 64)
        gated = gated_s[flat, :].reshape(8, OWN, LANES)
        grad = grad_s[flat, :].reshape(8, OWN, LANES)
        inner = rounded(inner_s[flat, :].reshape(8, OWN, LANES) + w[9] * gated)
        dgated = rounded(corr_s[flat, :].reshape(8, OWN, LANES) + w[9] * grad)
        dconv = (rounded(cot_s[at] * inner), dgated * conv_s[1, at], dgated * conv_s[0, at])
        terms = [dconv[s] * raw_s[3 * s + j, at] for s in range(3) for j in range(3)]
        terms.append(grad * gated)
        sums = tuple(total + jnp.sum(term, axis=0) for total, term in zip(sums, terms))
        firsts = []
        for value, off in ((dgated, 0), (inner, 256)):
            value = value.reshape(4, 2, OWN, LANES)
            firsts.append(value[:, 0])
            both = jnp.concatenate([value[:, 0], value[:, 1]], axis=2)
            for u in range(4):
                at = pl.ds(512 * u + off, 256)
                out_v[pl.ds(4 * i, 4), :, at] = both[:, 2 * u : 2 * u + 2].astype(BF16)
        edge_s[pl.ds(4 * i, 4)] = jnp.where(lane[:4] < 2, firsts[0], pltpu.roll(firsts[1], 2, axis=2))
        return sums

    zero = jnp.zeros((OWN, LANES), F32)
    edge_s[64] = zero
    sums = (zero,) * 10
    for g in range(4):
        sums = lax.fori_loop(4 * g, 4 * g + 4, finish, sums)
        part = (pl.ds(16 * g, 16), slice(None), pl.ds(0, TAIL))
        stores.append(copy(out_v.at[part], out.at[part], sems.at[9 + g]))
        stores[-1].start()
    totals = [jnp.sum(total, axis=1, keepdims=True) * scale for total in sums]
    dskip[...] = jnp.broadcast_to(totals[9], (OWN, LANES))

    spot = lax.broadcasted_iota(jnp.int32, (OWN, LANES), 1)
    pairs = lax.broadcasted_iota(jnp.int32, (OWN, LANES), 0) // 2
    spot = spot - 32 * pairs
    shared = zero
    for n in range(9):
        value = jnp.broadcast_to(totals[n], (OWN, LANES))
        high = rounded(value)
        mid = rounded(value - high)
        for base, piece in ((0, high), (9, mid), (18, value - high - mid)):
            shared = jnp.where(spot == base + n, piece, shared)
    for g in range(4):
        after = edge_s[pl.ds(16 * g + 1, 16)]
        extra = jnp.broadcast_to(shared[None], (16, OWN, LANES))
        for u in range(4):
            here = (pairs == u) & (spot >= 27) & (spot < 31)
            extra = jnp.where(here[None], pltpu.roll(after, 27 + 32 * u, axis=2), extra)
        extra = extra[:, 0:2] + extra[:, 2:4] + extra[:, 4:6] + extra[:, 6:8]
        out_v[16 * g : 16 * g + 16, :, TAIL:] = extra.astype(BF16)
    part = (slice(None), slice(None), pl.ds(TAIL, LANES))
    stores.append(copy(out_v.at[part], out.at[part], sems.at[13]))
    stores[-1].start()
    for store in stores:
        store.wait()


def cross_kernel(cross, tr, ti, last_back, first_back, out, rows):
    for p in range(OWN // 2):
        both = jnp.concatenate([cross[2 * p], cross[2 * p + 1]], axis=0)
        back = dot(wide(both), last_back[...])
        turn = jnp.concatenate(
            [turned_back(back[128 * i : 128 * i + 128], tr[...], ti[...]) for i in range(2)], axis=1
        )
        y = dot(first_back[...], tall(turn)) * (1.0 / 128.0)
        for i in range(2):
            rows[pl.ds(2 * p + i, ROWS, stride=OWN), :] = y[:, 128 * i : 128 * i + 128]
    for a in range(ROWS):
        out[:, 128 * a : 128 * a + 128] = rows[8 * a : 8 * a + 8, :]


def token_kernel(
    got, q, k, v, c, prev, nxt, w, mixed, dq, dk, dv, dshort
):
    for j in range(4):
        cols = slice(128 * j, 128 * j + 128)
        own = slice(16 * j, 16 * j + 16)

        def columns(off):
            parts = [got[own, :, 512 * u + off : 512 * u + off + 256] for u in range(4)]
            return jnp.concatenate([p.astype(F32) for p in parts], axis=1).reshape(128, 256).T

        dgated = columns(0)
        inner = columns(256)
        rest = got[own, :, TAIL : TAIL + 128].astype(F32)
        parts = [rest if u == 0 else pltpu.roll(rest, 128 - 32 * u, axis=2) for u in range(4)]
        extra = jnp.concatenate(parts, axis=1).reshape(128, 128).T
        for s in range(3):
            for n in range(3):
                at = 3 * s + n
                total = extra[at : at + 1] + extra[9 + at : 10 + at] + extra[18 + at : 19 + at]
                dshort[s, n : n + 1, cols] = total
        weight = [[w[s, n : n + 1, cols] for n in range(3)] for s in range(3)]
        cot = c[:, cols].astype(F32)
        cot_n = nxt[4:6, cols]

        def conv(seq, s):
            rows = seq.shape[0] - 2
            return (
                weight[s][0] * seq[2:] + weight[s][1] * seq[1 : 1 + rows] + weight[s][2] * seq[:rows]
            )

        def back(seq, s):
            total = (
                weight[s][0] * seq[:256] + weight[s][1] * seq[1:257] + weight[s][2] * seq[2:258]
            )
            return total.astype(BF16)

        q_ext = jnp.concatenate([prev[0:2, cols], q[:, cols].astype(F32)], axis=0)
        query = rounded(conv(q_ext, 0))
        mixed[:, cols] = (query * inner).astype(BF16)
        dconv = jnp.concatenate([rounded(cot * inner), rounded(cot_n * extra[29:31])], axis=0)
        dq[:, cols] = back(dconv, 0)
        dgated_ext = jnp.concatenate([dgated, extra[27:29]], axis=0)
        k_ext = jnp.concatenate([prev[2:4, cols], k[:, cols].astype(F32), nxt[0:2, cols]], axis=0)
        v_ext = jnp.concatenate([prev[4:6, cols], v[:, cols].astype(F32), nxt[2:4, cols]], axis=0)
        dk[:, cols] = back(dgated_ext * conv(v_ext, 2), 1)
        dv[:, cols] = back(dgated_ext * conv(k_ext, 1), 2)


def call(kernel, outs, ins, scratch=(), flops=0, moved=0, limit=24):
    shapes, specs = [o[0] for o in outs], [o[1] for o in outs]
    one = len(outs) == 1
    return pl.pallas_call(
        kernel,
        out_shape=shapes[0] if one else shapes,
        in_specs=list(ins),
        out_specs=specs[0] if one else specs,
        scratch_shapes=list(scratch),
        compiler_params=pltpu.CompilerParams(vmem_limit_bytes=limit << 20),
        cost_estimate=pl.CostEstimate(flops=flops, bytes_accessed=moved, transcendentals=0),
    )


def shape(*dims, kind=F32):
    return jax.ShapeDtypeStruct(dims, kind)


def pack():
    packed = shape(64, 16, 512, kind=BF16)
    stream = VMEM((256, 512), BF16)
    return call(
        pack_kernel, [(packed, HBM)], [HBM] * 4,
        [stream] * 4 + [VMEM((64, 16, 512), BF16), pltpu.SemaphoreType.DMA((8,))],
        moved=2 << 20, limit=60,
    )


def channels():
    big = VMEM((128, OWN, LANES), F32)
    flat = VMEM((1024, LANES), F32)
    spectra = VMEM((OWN, 128, 256), F32)
    return call(
        channel_kernel,
        [(shape(64, 2, TAIL + 128, kind=BF16), HBM), (shape(SPARE, 128, 256), HBM), (shape(OWN, LANES), WHOLE)],
        [WHOLE] * 2 + [HBM] + [WHOLE] * 6,
        [flat, flat, flat, flat, big, VMEM((2, 128, OWN, LANES), F32), VMEM((9, 128, OWN, LANES), F32),
         VMEM((65, OWN, LANES), F32), spectra, spectra, VMEM((64, 2, TAIL + 128), BF16),
         pltpu.SemaphoreType.DMA((14,))],
        flops=4 * 10**9, moved=4 << 20, limit=50,
    )


def body(query_in, key_in, value_in, short_weights, long_filter, skip_gain, cotangent):
    t = tables()
    turns = (t["turn_re"], t["turn_im"])
    count = lax.axis_size("ctx")

    tokens = shape(256, 512, kind=BF16)
    flat = VMEM((1024, LANES), F32)
    packed = pack()(query_in, key_in, value_in, cotangent)
    seqs = lax.all_to_all(packed, "ctx", split_axis=0, concat_axis=0, tiled=True)

    here = lax.axis_index("ctx").astype(jnp.int32).reshape(1)
    spectrum, own_w = call(
        filter_kernel,
        [(shape(SPARE, 128, 256), WHOLE), (shape(10, OWN, LANES), WHOLE)],
        [pl.BlockSpec(memory_space=pltpu.SMEM)] + [WHOLE] * 7, [flat],
        flops=10**9, moved=2 << 20, limit=60,
    )(here, long_filter, short_weights, skip_gain[:, None], t["first_three"], *turns, t["last"])

    ends = jnp.concatenate([query_in[254:], key_in[254:], value_in[254:]], axis=0)
    starts = jnp.concatenate([key_in[:2], value_in[:2], cotangent[:2]], axis=0)
    prev = lax.ppermute(ends, "ctx", [(i, i + 1) for i in range(count - 1)]).astype(F32)
    nxt = lax.ppermute(starts, "ctx", [(i + 1, i) for i in range(count - 1)]).astype(F32)

    answer, cross, dskip = channels()(
        seqs, own_w, spectrum, t["first_pair"], *turns, t["last"], t["last_back"], t["first_back"]
    )

    got = lax.all_to_all(answer, "ctx", split_axis=0, concat_axis=0, tiled=True)

    d_filter = call(
        cross_kernel, [(shape(OWN, 16384), WHOLE)], [WHOLE] * 5, [flat], flops=10**9, moved=2 << 20, limit=60
    )(cross, *turns, t["last_back"], t["first_back"])

    mixed, d_query, d_key, d_value, d_short = call(
        token_kernel, [(tokens, WHOLE)] * 4 + [(shape(3, 3, 512), WHOLE)], [WHOLE] * 8, moved=3 << 20
    )(got, query_in, key_in, value_in, cotangent, prev, nxt, short_weights)
    return (mixed, d_query, d_key, d_value, d_filter, dskip[:, 0], d_short)


def solution(mesh):
    tokens = P("ctx", "tp")
    rows = P(("tp", "ctx"), None)
    taps = P(None, None, "tp")
    flat = P(("tp", "ctx"))
    in_specs = (tokens, tokens, tokens, taps, rows, flat, tokens)
    out_specs = (tokens, tokens, tokens, tokens, rows, flat, taps)
    return jax.shard_map(body, mesh=mesh, in_specs=in_specs, out_specs=out_specs, check_vma=False)
```

```python
import jax
import jax.numpy as jnp
import ml_dtypes
import numpy as np
from jax import lax
from jax.experimental import pallas as pl
from jax.experimental.pallas import tpu as pltpu
from jax.sharding import PartitionSpec as P

ROWS = 128
COLS = 128
LANES = 128
OWN = 8
F32 = jnp.float32
BF16 = jnp.bfloat16
VMEM = pltpu.VMEM
HBM = pl.BlockSpec(memory_space=pltpu.HBM)
WHOLE = pl.BlockSpec(memory_space=pltpu.VMEM)
GROUP = 8
SPARE = 24
TAIL = 2048


def halves(table):
    high = table.astype(np.float32).astype(ml_dtypes.bfloat16)
    low = (table - high.astype(np.float64)).astype(np.float32).astype(ml_dtypes.bfloat16)
    return high, low


def tables():
    r = np.arange(128, dtype=np.int64)
    full = 4 * ROWS * COLS
    first = 2.0 * np.pi / 512 * ((r[None, :] * (2 * r[:, None] + 1)) % 512)
    turn = -2.0 * np.pi / full * ((r[None, :] * (2 * r[:, None] + 1)) % full)
    last = 2.0 * np.pi / 128 * ((r[:, None] * r[None, :]) % 128)
    w_high, w_low = halves(np.concatenate([np.cos(first), -np.sin(first)], 0))
    t = np.block([[np.cos(last), -np.sin(last)], [np.sin(last), np.cos(last)]])
    t_high, t_low = halves(t)
    i_high, i_low = halves(t.T.copy())
    back = np.concatenate([np.cos(first).T, -np.sin(first).T], 1) * (2.0 / (2 * ROWS * COLS))
    b_high, b_low = halves(back)
    return dict(
        first_pair=np.concatenate([w_high, w_low], 1),
        first_three=np.concatenate([w_high, w_low, w_high], 1),
        turn_re=np.cos(turn).astype(np.float32),
        turn_im=np.sin(turn).astype(np.float32),
        last=np.concatenate([t_high, t_high, t_low], 0),
        last_back=np.concatenate([i_high, i_high, i_low], 0),
        first_back=np.concatenate([b_high, b_low, b_high], 1),
    )


def dot(a, b):
    return jnp.dot(a, b, preferred_element_type=F32)


def split(x):
    high = x.astype(BF16)
    return high, (x - high.astype(F32)).astype(BF16)


def rounded(x):
    return x.astype(BF16).astype(F32)


def wide(x):
    high, low = split(x)
    return jnp.concatenate([high, low, high], axis=1)


def tall(x):
    high, low = split(x)
    return jnp.concatenate([high, high, low], axis=0)


def turned(part, tr, ti):
    re, im = part[:128], part[128:]
    return jnp.concatenate([re * tr - im * ti, re * ti + im * tr], axis=1)


def turned_back(part, tr, ti):
    re, im = part[:, :128], part[:, 128:]
    return jnp.concatenate([re * tr + im * ti, im * tr - re * ti], axis=0)


def copy(source, target, sem):
    return pltpu.make_async_copy(source, target, sem)


def pack_kernel(q, k, v, c, out, q_v, k_v, v_v, c_v, out_v, sems):
    loads = [copy(a, b, sems.at[i]) for i, (a, b) in enumerate(((k, k_v), (q, q_v), (v, v_v), (c, c_v)))]
    for load in loads:
        load.start()
    stores = []
    for load in loads:
        load.wait()
    for j in range(4):
        cols = slice(128 * j, 128 * j + 128)
        for top, low, off in ((k_v, q_v, 0), (v_v, c_v, 256)):
            upper = top[:, cols].T.astype(F32).reshape(16, OWN, 256)
            lower = low[:, cols].T.astype(F32).reshape(16, OWN, 256)
            both = jnp.concatenate([upper, lower], axis=1)
            out_v[16 * j : 16 * j + 16, :, off : off + 256] = both.astype(BF16)
        part = pl.ds(16 * j, 16)
        stores.append(copy(out_v.at[part], out.at[part], sems.at[4 + j]))
        stores[j].start()
    for store in stores:
        store.wait()


def weight_kernel(here, w, skip, after, own_w):
    wanted = OWN * here[0] + lax.broadcasted_iota(jnp.int32, (OWN, 512), 0)
    mine = lax.broadcasted_iota(jnp.int32, (OWN, 512), 1) == wanted
    for s in range(3):
        for n in range(3):
            value = jnp.sum(jnp.where(mine, w[s, n : n + 1, :], 0.0), axis=1, keepdims=True)
            own_w[3 * s + n] = jnp.broadcast_to(value, (OWN, LANES))
    own_w[9] = jnp.broadcast_to(skip[...], (OWN, LANES))


def filter_kernel(f, first, tr, ti, last, out, rows):
    for a in range(ROWS):
        rows[8 * a : 8 * a + 8, :] = f[:, 128 * a : 128 * a + 128]
    for p in range(OWN // 2):
        x = jnp.concatenate(
            [rows[pl.ds(2 * p + i, ROWS, stride=OWN), :] for i in range(2)], axis=1
        )
        part = dot(first[...], tall(x))
        lhs = jnp.concatenate(
            [turned(part[:, 128 * i : 128 * i + 128], tr[...], ti[...]) for i in range(2)], axis=0
        )
        spec = dot(wide(lhs), last[...])
        out[2 * p] = spec[:128]
        out[2 * p + 1] = spec[128:]


def lagged(x, lane, by):
    r = pltpu.roll(x, by, axis=2)
    return jnp.where(lane < by, r[1:9], r[2:10])


def channel_kernel(
    x, w, filt, first, tr, ti, last, last_back, first_back,
    out, cross, dskip,
    gated_s, grad_s, inner_s, corr_s, cot_s, conv_s, raw_s, edge_s, filt_v, cross_v, out_v, sems,
):
    load = copy(filt.at[pl.ds(0, OWN)], filt_v, sems.at[0])
    load.start()
    lane = lax.broadcasted_iota(jnp.int32, (8, OWN, LANES), 2)
    scale = 1.0 / 128.0

    def blocks(value, upper, off):
        rows = slice(0, 8) if upper else slice(8, 16)
        lo = value[:, rows, off : off + 128]
        hi = value[:, rows, off + 128 : off + 256]
        return jnp.stack([lo, hi], axis=1).reshape(-1, OWN, LANES)

    def convolve(i, carry):
        s0 = 4 * i
        keep = jnp.where(i > 0, 1.0, 0.0).astype(F32)
        before = x[pl.ds(jnp.maximum(s0 - 1, 0), 1)].astype(F32) * keep
        here = x[pl.ds(s0, 4)].astype(F32)
        value = jnp.concatenate([before, here], axis=0)
        at = pl.ds(8 * i, 8)
        convs = []
        for s, (upper, off) in enumerate(((False, 0), (True, 0), (True, 256))):
            seq = blocks(value, upper, off)
            lags = [seq[2:], lagged(seq, lane, 1), lagged(seq, lane, 2)]
            for j in range(3):
                raw_s[3 * s + j, at] = lags[j]
            convs.append(
                w[3 * s] * lags[0] + w[3 * s + 1] * lags[1] + w[3 * s + 2] * lags[2]
            )
        cot = blocks(here, False, 256)
        cot_s[at] = cot
        conv_s[0, at] = convs[1]
        conv_s[1, at] = convs[2]
        flat = pl.ds(64 * i, 64)
        gated_s[flat, :] = rounded(convs[1] * convs[2]).reshape(64, LANES)
        grad_s[flat, :] = rounded(cot * rounded(convs[0])).reshape(64, LANES)
        return carry

    lax.fori_loop(0, 16, convolve, 0, unroll=4)

    load.wait()
    stores = []
    for g in range(OWN // GROUP):
        chans = range(GROUP * g, GROUP * g + GROUP)
        lhs = []
        for ch in chans:
            own = pl.ds(ch, ROWS, stride=OWN)
            pair = jnp.concatenate([gated_s[own, :], grad_s[own, :]], axis=1).astype(BF16)
            part = dot(first[...], jnp.concatenate([pair, pair], axis=0))
            lhs += [turned(part[:, 128 * i : 128 * i + 128], tr[...], ti[...]) for i in range(2)]
        specs = dot(wide(jnp.concatenate(lhs, axis=0)), last[...])
        lhs = []
        for n, ch in enumerate(chans):
            spec = specs[256 * n : 256 * n + 256]
            gr, gi = spec[:128, :128], spec[:128, 128:]
            dr, di = spec[128:, :128], spec[128:, 128:]
            fr, fi = filt_v[ch][:, :128], filt_v[ch][:, 128:]
            cross_v[ch] = jnp.concatenate([gr * dr + gi * di, gr * di - gi * dr], axis=1)
            lhs.append(jnp.concatenate([gr * fr - gi * fi, gr * fi + gi * fr], axis=1))
            lhs.append(jnp.concatenate([fr * dr + fi * di, fr * di - fi * dr], axis=1))
        backs = dot(wide(jnp.concatenate(lhs, axis=0)), last_back[...])
        for n, ch in enumerate(chans):
            own = pl.ds(ch, ROWS, stride=OWN)
            back = backs[256 * n : 256 * n + 256]
            turn = jnp.concatenate(
                [turned_back(back[128 * i : 128 * i + 128], tr[...], ti[...]) for i in range(2)], axis=1
            )
            y = dot(first_back[...], tall(turn))
            inner_s[own, :] = y[:, :128]
            corr_s[own, :] = y[:, 128:]
        part = pl.ds(GROUP * g, GROUP)
        stores.append(copy(cross_v.at[part], cross.at[part], sems.at[1 + g]))
        stores[g].start()

    def finish(i, sums):
        at = pl.ds(8 * i, 8)
        flat = pl.ds(64 * i, 64)
        gated = gated_s[flat, :].reshape(8, OWN, LANES)
        grad = grad_s[flat, :].reshape(8, OWN, LANES)
        inner = rounded(inner_s[flat, :].reshape(8, OWN, LANES) + w[9] * gated)
        dgated = rounded(corr_s[flat, :].reshape(8, OWN, LANES) + w[9] * grad)
        dconv = (rounded(cot_s[at] * inner), dgated * conv_s[1, at], dgated * conv_s[0, at])
        terms = [dconv[s] * raw_s[3 * s + j, at] for s in range(3) for j in range(3)]
        terms.append(grad * gated)
        sums = tuple(total + jnp.sum(term, axis=0) for total, term in zip(sums, terms))
        firsts = []
        for value, off in ((dgated, 0), (inner, 256)):
            value = value.reshape(4, 2, OWN, LANES)
            firsts.append(value[:, 0])
            both = jnp.concatenate([value[:, 0], value[:, 1]], axis=2)
            for u in range(4):
                at = pl.ds(512 * u + off, 256)
                out_v[pl.ds(4 * i, 4), :, at] = both[:, 2 * u : 2 * u + 2].astype(BF16)
        edge_s[pl.ds(4 * i, 4)] = jnp.where(lane[:4] < 2, firsts[0], pltpu.roll(firsts[1], 2, axis=2))
        return sums

    zero = jnp.zeros((OWN, LANES), F32)
    edge_s[64] = zero
    sums = (zero,) * 10
    for g in range(4):
        sums = lax.fori_loop(4 * g, 4 * g + 4, finish, sums, unroll=4)
        part = (pl.ds(16 * g, 16), slice(None), pl.ds(0, TAIL))
        stores.append(copy(out_v.at[part], out.at[part], sems.at[9 + g]))
        stores[-1].start()
    totals = [jnp.sum(total, axis=1, keepdims=True) * scale for total in sums]
    dskip[...] = jnp.broadcast_to(totals[9], (OWN, LANES))

    spot = lax.broadcasted_iota(jnp.int32, (OWN, LANES), 1)
    pairs = lax.broadcasted_iota(jnp.int32, (OWN, LANES), 0) // 2
    spot = spot - 32 * pairs
    shared = zero
    for n in range(9):
        value = jnp.broadcast_to(totals[n], (OWN, LANES))
        high = rounded(value)
        mid = rounded(value - high)
        for base, piece in ((0, high), (9, mid), (18, value - high - mid)):
            shared = jnp.where(spot == base + n, piece, shared)
    for g in range(4):
        after = edge_s[pl.ds(16 * g + 1, 16)]
        extra = jnp.broadcast_to(shared[None], (16, OWN, LANES))
        for u in range(4):
            here = (pairs == u) & (spot >= 27) & (spot < 31)
            extra = jnp.where(here[None], pltpu.roll(after, 27 + 32 * u, axis=2), extra)
        extra = extra[:, 0:2] + extra[:, 2:4] + extra[:, 4:6] + extra[:, 6:8]
        out_v[16 * g : 16 * g + 16, :, TAIL:] = extra.astype(BF16)
    part = (slice(None), slice(None), pl.ds(TAIL, LANES))
    stores.append(copy(out_v.at[part], out.at[part], sems.at[13]))
    stores[-1].start()
    for store in stores:
        store.wait()


def cross_kernel(cross, tr, ti, last_back, first_back, out, rows):
    for p in range(OWN // 2):
        both = jnp.concatenate([cross[2 * p], cross[2 * p + 1]], axis=0)
        back = dot(wide(both), last_back[...])
        turn = jnp.concatenate(
            [turned_back(back[128 * i : 128 * i + 128], tr[...], ti[...]) for i in range(2)], axis=1
        )
        y = dot(first_back[...], tall(turn)) * (1.0 / 128.0)
        for i in range(2):
            rows[pl.ds(2 * p + i, ROWS, stride=OWN), :] = y[:, 128 * i : 128 * i + 128]
    for a in range(ROWS):
        out[:, 128 * a : 128 * a + 128] = rows[8 * a : 8 * a + 8, :]


def conv_kernel(q, k, v, prev, nxt, w, query, ck, cv):
    for j in range(4):
        cols = slice(128 * j, 128 * j + 128)

        def conv(parts, s):
            seq = jnp.concatenate(parts, axis=0)
            rows = seq.shape[0] - 2
            tap = [w[s, n : n + 1, cols] for n in range(3)]
            return tap[0] * seq[2:] + tap[1] * seq[1 : 1 + rows] + tap[2] * seq[:rows]

        query[:, cols] = conv([prev[0:2, cols], q[:, cols].astype(F32)], 0).astype(BF16)
        ck[0:258, cols] = conv([prev[2:4, cols], k[:, cols].astype(F32), nxt[0:2, cols]], 1)
        cv[0:258, cols] = conv([prev[4:6, cols], v[:, cols].astype(F32), nxt[2:4, cols]], 2)


def token_kernel(got, query, ck, cv, c, nxt, w, mixed, dq, dk, dv, dshort, stage):
    for j in range(4):
        cols = slice(128 * j, 128 * j + 128)
        own = slice(16 * j, 16 * j + 16)

        def columns(off):
            parts = [got[own, :, 512 * u + off : 512 * u + off + 256] for u in range(4)]
            return jnp.concatenate([p.astype(F32) for p in parts], axis=1).reshape(128, 256).T

        rest = got[own, :, TAIL : TAIL + 128].astype(F32)
        parts = [rest if u == 0 else pltpu.roll(rest, 128 - 32 * u, axis=2) for u in range(4)]
        extra = jnp.concatenate(parts, axis=1).reshape(128, 128).T
        for s in range(3):
            for n in range(3):
                at = 3 * s + n
                total = extra[at : at + 1] + extra[9 + at : 10 + at] + extra[18 + at : 19 + at]
                dshort[s, n : n + 1, cols] = total

        def back(s):
            seq = stage.at[j, s]
            tap = [w[s, n : n + 1, cols] for n in range(3)]
            total = tap[0] * seq[0:256, :] + tap[1] * seq[1:257, :] + tap[2] * seq[2:258, :]
            return total.astype(BF16)

        inner = columns(256)
        mixed[:, cols] = (query[:, cols].astype(F32) * inner).astype(BF16)
        stage[j, 0, 0:256, :] = rounded(c[:, cols].astype(F32) * inner)
        stage[j, 0, 256:258, :] = rounded(nxt[4:6, cols] * extra[29:31])
        dq[:, cols] = back(0)
        dgated = columns(0)
        stage[j, 1, 0:256, :] = dgated * cv[0:256, cols]
        stage[j, 1, 256:258, :] = extra[27:29] * cv[256:258, cols]
        dk[:, cols] = back(1)
        stage[j, 2, 0:256, :] = dgated * ck[0:256, cols]
        stage[j, 2, 256:258, :] = extra[27:29] * ck[256:258, cols]
        dv[:, cols] = back(2)


def call(kernel, outs, ins, scratch=(), flops=0, moved=0, limit=24):
    shapes, specs = [o[0] for o in outs], [o[1] for o in outs]
    one = len(outs) == 1
    return pl.pallas_call(
        kernel,
        out_shape=shapes[0] if one else shapes,
        in_specs=list(ins),
        out_specs=specs[0] if one else specs,
        scratch_shapes=list(scratch),
        compiler_params=pltpu.CompilerParams(vmem_limit_bytes=limit << 20),
        cost_estimate=pl.CostEstimate(flops=flops, bytes_accessed=moved, transcendentals=0),
    )


def shape(*dims, kind=F32):
    return jax.ShapeDtypeStruct(dims, kind)


def pack():
    packed = shape(64, 16, 512, kind=BF16)
    stream = VMEM((256, 512), BF16)
    return call(
        pack_kernel, [(packed, HBM)], [HBM] * 4,
        [stream] * 4 + [VMEM((64, 16, 512), BF16), pltpu.SemaphoreType.DMA((8,))],
        moved=2 << 20, limit=60,
    )


def channels():
    big = VMEM((128, OWN, LANES), F32)
    flat = VMEM((1024, LANES), F32)
    spectra = VMEM((OWN, 128, 256), F32)
    return call(
        channel_kernel,
        [(shape(64, 2, TAIL + 128, kind=BF16), HBM), (shape(SPARE, 128, 256), HBM), (shape(OWN, LANES), WHOLE)],
        [WHOLE] * 2 + [HBM] + [WHOLE] * 6,
        [flat, flat, flat, flat, big, VMEM((2, 128, OWN, LANES), F32), VMEM((9, 128, OWN, LANES), F32),
         VMEM((65, OWN, LANES), F32), spectra, spectra, VMEM((64, 2, TAIL + 128), BF16),
         pltpu.SemaphoreType.DMA((14,))],
        flops=4 * 10**9, moved=4 << 20, limit=50,
    )


def body(query_in, key_in, value_in, short_weights, long_filter, skip_gain, cotangent):
    t = tables()
    turns = (t["turn_re"], t["turn_im"])
    count = lax.axis_size("ctx")

    tokens = shape(256, 512, kind=BF16)
    flat = VMEM((1024, LANES), F32)
    packed = pack()(query_in, key_in, value_in, cotangent)
    seqs = lax.all_to_all(packed, "ctx", split_axis=0, concat_axis=0, tiled=True)

    here = lax.axis_index("ctx").astype(jnp.int32).reshape(1)
    spectrum = call(
        filter_kernel, [(shape(SPARE, 128, 256), WHOLE)], [WHOLE] * 5, [flat],
        flops=10**9, moved=2 << 20, limit=60,
    )(long_filter, t["first_three"], *turns, t["last"])
    own_w = call(
        weight_kernel, [(shape(10, OWN, LANES), WHOLE)],
        [pl.BlockSpec(memory_space=pltpu.SMEM), WHOLE, WHOLE, HBM], moved=1 << 20,
    )(here, short_weights, skip_gain[:, None], spectrum)

    ends = jnp.concatenate([query_in[254:], key_in[254:], value_in[254:]], axis=0)
    starts = jnp.concatenate([key_in[:2], value_in[:2], cotangent[:2]], axis=0)
    prev = lax.ppermute(ends, "ctx", [(i, i + 1) for i in range(count - 1)]).astype(F32)
    nxt = lax.ppermute(starts, "ctx", [(i + 1, i) for i in range(count - 1)]).astype(F32)

    answer, cross, dskip = channels()(
        seqs, own_w, spectrum, t["first_pair"], *turns, t["last"], t["last_back"], t["first_back"]
    )

    got = lax.all_to_all(answer, "ctx", split_axis=0, concat_axis=0, tiled=True)

    d_filter = call(
        cross_kernel, [(shape(OWN, 16384), WHOLE)], [WHOLE] * 5, [flat], flops=10**9, moved=2 << 20, limit=60
    )(cross, *turns, t["last_back"], t["first_back"])

    extended = shape(264, 512)
    query, conv_k, conv_v = call(
        conv_kernel, [(tokens, WHOLE), (extended, WHOLE), (extended, WHOLE)], [WHOLE] * 6, moved=2 << 20
    )(query_in, key_in, value_in, prev, nxt, short_weights)
    mixed, d_query, d_key, d_value, d_short = call(
        token_kernel, [(tokens, WHOLE)] * 4 + [(shape(3, 3, 512), WHOLE)], [WHOLE] * 7,
        [VMEM((4, 3, 264, LANES), F32)], moved=3 << 20,
    )(got, query, conv_k, conv_v, cotangent, nxt, short_weights)
    return (mixed, d_query, d_key, d_value, d_filter, dskip[:, 0], d_short)


def solution(mesh):
    tokens = P("ctx", "tp")
    rows = P(("tp", "ctx"), None)
    taps = P(None, None, "tp")
    flat = P(("tp", "ctx"))
    in_specs = (tokens, tokens, tokens, taps, rows, flat, tokens)
    out_specs = (tokens, tokens, tokens, tokens, rows, flat, taps)
    return jax.shard_map(body, mesh=mesh, in_specs=in_specs, out_specs=out_specs, check_vma=False)
```

```python
import jax
import jax.numpy as jnp
import ml_dtypes
import numpy as np
from jax import lax
from jax.experimental import pallas as pl
from jax.experimental.pallas import tpu as pltpu
from jax.sharding import PartitionSpec as P

ROWS = 128
COLS = 128
LANES = 128
OWN = 8
F32 = jnp.float32
BF16 = jnp.bfloat16
VMEM = pltpu.VMEM
HBM = pl.BlockSpec(memory_space=pltpu.HBM)
WHOLE = pl.BlockSpec(memory_space=pltpu.VMEM)
GROUP = 8
SPARE = 24
TAIL = 2048


def halves(table):
    high = table.astype(np.float32).astype(ml_dtypes.bfloat16)
    low = (table - high.astype(np.float64)).astype(np.float32).astype(ml_dtypes.bfloat16)
    return high, low


def tables():
    r = np.arange(128, dtype=np.int64)
    full = 4 * ROWS * COLS
    first = 2.0 * np.pi / 512 * ((r[None, :] * (2 * r[:, None] + 1)) % 512)
    turn = -2.0 * np.pi / full * ((r[None, :] * (2 * r[:, None] + 1)) % full)
    last = 2.0 * np.pi / 128 * ((r[:, None] * r[None, :]) % 128)
    w_high, w_low = halves(np.concatenate([np.cos(first), -np.sin(first)], 0))
    t = np.block([[np.cos(last), -np.sin(last)], [np.sin(last), np.cos(last)]])
    t_high, t_low = halves(t)
    i_high, i_low = halves(t.T.copy())
    back = np.concatenate([np.cos(first).T, -np.sin(first).T], 1) * (2.0 / (2 * ROWS * COLS))
    b_high, b_low = halves(back)
    return dict(
        first_pair=np.concatenate([w_high, w_low], 1),
        first_three=np.concatenate([w_high, w_low, w_high], 1),
        turn_re=np.cos(turn).astype(np.float32),
        turn_im=np.sin(turn).astype(np.float32),
        last=np.concatenate([t_high, t_high, t_low], 0),
        last_back=np.concatenate([i_high, i_high, i_low], 0),
        first_back=np.concatenate([b_high, b_low, b_high], 1),
    )


def dot(a, b):
    return jnp.dot(a, b, preferred_element_type=F32)


def split(x):
    high = x.astype(BF16)
    return high, (x - high.astype(F32)).astype(BF16)


def rounded(x):
    return x.astype(BF16).astype(F32)


def wide(x):
    high, low = split(x)
    return jnp.concatenate([high, low, high], axis=1)


def tall(x):
    high, low = split(x)
    return jnp.concatenate([high, high, low], axis=0)


def turned(part, tr, ti):
    re, im = part[:128], part[128:]
    return jnp.concatenate([re * tr - im * ti, re * ti + im * tr], axis=1)


def turned_back(part, tr, ti):
    re, im = part[:, :128], part[:, 128:]
    return jnp.concatenate([re * tr + im * ti, im * tr - re * ti], axis=0)


def copy(source, target, sem):
    return pltpu.make_async_copy(source, target, sem)


def pack_kernel(q, k, v, c, out, q_v, k_v, v_v, c_v, out_v, sems):
    loads = [copy(a, b, sems.at[i]) for i, (a, b) in enumerate(((k, k_v), (q, q_v), (v, v_v), (c, c_v)))]
    for load in loads:
        load.start()
    stores = []
    for load in loads:
        load.wait()
    for j in range(4):
        cols = slice(128 * j, 128 * j + 128)
        for top, low, off in ((k_v, q_v, 0), (v_v, c_v, 256)):
            upper = top[:, cols].T.astype(F32).reshape(16, OWN, 256)
            lower = low[:, cols].T.astype(F32).reshape(16, OWN, 256)
            both = jnp.concatenate([upper, lower], axis=1)
            out_v[16 * j : 16 * j + 16, :, off : off + 256] = both.astype(BF16)
        part = pl.ds(16 * j, 16)
        stores.append(copy(out_v.at[part], out.at[part], sems.at[4 + j]))
        stores[j].start()
    for store in stores:
        store.wait()


def weight_kernel(here, w, skip, after, own_w):
    wanted = OWN * here[0] + lax.broadcasted_iota(jnp.int32, (OWN, 512), 0)
    mine = lax.broadcasted_iota(jnp.int32, (OWN, 512), 1) == wanted
    for s in range(3):
        for n in range(3):
            value = jnp.sum(jnp.where(mine, w[s, n : n + 1, :], 0.0), axis=1, keepdims=True)
            own_w[3 * s + n] = jnp.broadcast_to(value, (OWN, LANES))
    own_w[9] = jnp.broadcast_to(skip[...], (OWN, LANES))


def filter_kernel(f, first, tr, ti, last, out, rows):
    for a in range(ROWS):
        rows[8 * a : 8 * a + 8, :] = f[:, 128 * a : 128 * a + 128]
    for p in range(OWN // 2):
        x = jnp.concatenate(
            [rows[pl.ds(2 * p + i, ROWS, stride=OWN), :] for i in range(2)], axis=1
        )
        part = dot(first[...], tall(x))
        lhs = jnp.concatenate(
            [turned(part[:, 128 * i : 128 * i + 128], tr[...], ti[...]) for i in range(2)], axis=0
        )
        spec = dot(wide(lhs), last[...])
        out[2 * p] = spec[:128]
        out[2 * p + 1] = spec[128:]


def lagged(x, lane, by):
    r = pltpu.roll(x, by, axis=2)
    return jnp.where(lane < by, r[1:9], r[2:10])


def channel_kernel(
    x, w, filt, first, tr, ti, last, last_back, first_back,
    out, cross, dskip,
    gated_s, grad_s, inner_s, corr_s, cot_s, conv_s, raw_s, edge_s, filt_v, cross_v, out_v, sems,
):
    load = copy(filt.at[pl.ds(0, OWN)], filt_v, sems.at[0])
    load.start()
    lane = lax.broadcasted_iota(jnp.int32, (8, OWN, LANES), 2)
    scale = 1.0 / 128.0

    def blocks(value, upper, off):
        rows = slice(0, 8) if upper else slice(8, 16)
        lo = value[:, rows, off : off + 128]
        hi = value[:, rows, off + 128 : off + 256]
        return jnp.stack([lo, hi], axis=1).reshape(-1, OWN, LANES)

    def convolve(i, carry):
        s0 = 4 * i
        keep = jnp.where(i > 0, 1.0, 0.0).astype(F32)
        before = x[pl.ds(jnp.maximum(s0 - 1, 0), 1)].astype(F32) * keep
        here = x[pl.ds(s0, 4)].astype(F32)
        value = jnp.concatenate([before, here], axis=0)
        at = pl.ds(8 * i, 8)
        convs = []
        for s, (upper, off) in enumerate(((False, 0), (True, 0), (True, 256))):
            seq = blocks(value, upper, off)
            lags = [seq[2:], lagged(seq, lane, 1), lagged(seq, lane, 2)]
            for j in range(3):
                raw_s[3 * s + j, at] = lags[j]
            convs.append(
                w[3 * s] * lags[0] + w[3 * s + 1] * lags[1] + w[3 * s + 2] * lags[2]
            )
        cot = blocks(here, False, 256)
        cot_s[at] = cot
        conv_s[0, at] = convs[1]
        conv_s[1, at] = convs[2]
        flat = pl.ds(64 * i, 64)
        gated_s[flat, :] = rounded(convs[1] * convs[2]).reshape(64, LANES)
        grad_s[flat, :] = rounded(cot * rounded(convs[0])).reshape(64, LANES)
        return carry

    lax.fori_loop(0, 16, convolve, 0, unroll=4)

    load.wait()
    stores = []
    for g in range(OWN // GROUP):
        chans = range(GROUP * g, GROUP * g + GROUP)
        lhs = []
        for ch in chans:
            own = pl.ds(ch, ROWS, stride=OWN)
            pair = jnp.concatenate([gated_s[own, :], grad_s[own, :]], axis=1).astype(BF16)
            part = dot(first[...], jnp.concatenate([pair, pair], axis=0))
            lhs += [turned(part[:, 128 * i : 128 * i + 128], tr[...], ti[...]) for i in range(2)]
        specs = dot(wide(jnp.concatenate(lhs, axis=0)), last[...])
        lhs = []
        for n, ch in enumerate(chans):
            spec = specs[256 * n : 256 * n + 256]
            gr, gi = spec[:128, :128], spec[:128, 128:]
            dr, di = spec[128:, :128], spec[128:, 128:]
            fr, fi = filt_v[ch][:, :128], filt_v[ch][:, 128:]
            cross_v[ch] = jnp.concatenate([gr * dr + gi * di, gr * di - gi * dr], axis=1)
            lhs.append(jnp.concatenate([gr * fr - gi * fi, gr * fi + gi * fr], axis=1))
            lhs.append(jnp.concatenate([fr * dr + fi * di, fr * di - fi * dr], axis=1))
        backs = dot(wide(jnp.concatenate(lhs, axis=0)), last_back[...])
        for n, ch in enumerate(chans):
            own = pl.ds(ch, ROWS, stride=OWN)
            back = backs[256 * n : 256 * n + 256]
            turn = jnp.concatenate(
                [turned_back(back[128 * i : 128 * i + 128], tr[...], ti[...]) for i in range(2)], axis=1
            )
            y = dot(first_back[...], tall(turn))
            inner_s[own, :] = y[:, :128]
            corr_s[own, :] = y[:, 128:]
        part = pl.ds(GROUP * g, GROUP)
        stores.append(copy(cross_v.at[part], cross.at[part], sems.at[1 + g]))
        stores[g].start()

    def finish(i, sums):
        at = pl.ds(8 * i, 8)
        flat = pl.ds(64 * i, 64)
        gated = gated_s[flat, :].reshape(8, OWN, LANES)
        grad = grad_s[flat, :].reshape(8, OWN, LANES)
        inner = rounded(inner_s[flat, :].reshape(8, OWN, LANES) + w[9] * gated)
        dgated = rounded(corr_s[flat, :].reshape(8, OWN, LANES) + w[9] * grad)
        dconv = (rounded(cot_s[at] * inner), dgated * conv_s[1, at], dgated * conv_s[0, at])
        terms = [dconv[s] * raw_s[3 * s + j, at] for s in range(3) for j in range(3)]
        terms.append(grad * gated)
        sums = tuple(total + jnp.sum(term, axis=0) for total, term in zip(sums, terms))
        firsts = []
        for value, off in ((dgated, 0), (inner, 256)):
            value = value.reshape(4, 2, OWN, LANES)
            firsts.append(value[:, 0])
            both = jnp.concatenate([value[:, 0], value[:, 1]], axis=2)
            for u in range(4):
                at = pl.ds(512 * u + off, 256)
                out_v[pl.ds(4 * i, 4), :, at] = both[:, 2 * u : 2 * u + 2].astype(BF16)
        edge_s[pl.ds(4 * i, 4)] = jnp.where(lane[:4] < 2, firsts[0], pltpu.roll(firsts[1], 2, axis=2))
        return sums

    zero = jnp.zeros((OWN, LANES), F32)
    edge_s[64] = zero
    sums = (zero,) * 10
    for g in range(4):
        sums = lax.fori_loop(4 * g, 4 * g + 4, finish, sums, unroll=4)
        part = (pl.ds(16 * g, 16), slice(None), pl.ds(0, TAIL))
        stores.append(copy(out_v.at[part], out.at[part], sems.at[9 + g]))
        stores[-1].start()
    totals = [jnp.sum(total, axis=1, keepdims=True) * scale for total in sums]
    dskip[...] = jnp.broadcast_to(totals[9], (OWN, LANES))

    spot = lax.broadcasted_iota(jnp.int32, (OWN, LANES), 1)
    pairs = lax.broadcasted_iota(jnp.int32, (OWN, LANES), 0) // 2
    spot = spot - 32 * pairs
    shared = zero
    for n in range(9):
        value = jnp.broadcast_to(totals[n], (OWN, LANES))
        high = rounded(value)
        mid = rounded(value - high)
        for base, piece in ((0, high), (9, mid), (18, value - high - mid)):
            shared = jnp.where(spot == base + n, piece, shared)
    for g in range(4):
        after = edge_s[pl.ds(16 * g + 1, 16)]
        extra = jnp.broadcast_to(shared[None], (16, OWN, LANES))
        for u in range(4):
            here = (pairs == u) & (spot >= 27) & (spot < 31)
            extra = jnp.where(here[None], pltpu.roll(after, 27 + 32 * u, axis=2), extra)
        extra = extra[:, 0:2] + extra[:, 2:4] + extra[:, 4:6] + extra[:, 6:8]
        out_v[16 * g : 16 * g + 16, :, TAIL:] = extra.astype(BF16)
    part = (slice(None), slice(None), pl.ds(TAIL, LANES))
    stores.append(copy(out_v.at[part], out.at[part], sems.at[13]))
    stores[-1].start()
    for store in stores:
        store.wait()


def cross_kernel(cross, tr, ti, last_back, first_back, out, rows):
    for p in range(OWN // 2):
        both = jnp.concatenate([cross[2 * p], cross[2 * p + 1]], axis=0)
        back = dot(wide(both), last_back[...])
        turn = jnp.concatenate(
            [turned_back(back[128 * i : 128 * i + 128], tr[...], ti[...]) for i in range(2)], axis=1
        )
        y = dot(first_back[...], tall(turn)) * (1.0 / 128.0)
        for i in range(2):
            rows[pl.ds(2 * p + i, ROWS, stride=OWN), :] = y[:, 128 * i : 128 * i + 128]
    for a in range(ROWS):
        out[:, 128 * a : 128 * a + 128] = rows[8 * a : 8 * a + 8, :]


def conv_kernel(q, k, v, prev, nxt, w, query, ck, cv):
    for j in range(4):
        cols = slice(128 * j, 128 * j + 128)

        def conv(parts, s):
            seq = jnp.concatenate(parts, axis=0)
            rows = seq.shape[0] - 2
            tap = [w[s, n : n + 1, cols] for n in range(3)]
            return tap[0] * seq[2:] + tap[1] * seq[1 : 1 + rows] + tap[2] * seq[:rows]

        query[:, cols] = conv([prev[0:2, cols], q[:, cols].astype(F32)], 0).astype(BF16)
        ck[0:258, cols] = conv([prev[2:4, cols], k[:, cols].astype(F32), nxt[0:2, cols]], 1)
        cv[0:258, cols] = conv([prev[4:6, cols], v[:, cols].astype(F32), nxt[2:4, cols]], 2)


def token_kernel(got, query, ck, cv, c, nxt, w, mixed, dq, dk, dv, dshort, stage):
    for j in range(4):
        cols = slice(128 * j, 128 * j + 128)
        own = slice(16 * j, 16 * j + 16)

        def columns(off):
            parts = [got[own, :, 512 * u + off : 512 * u + off + 256] for u in range(4)]
            return jnp.concatenate([p.astype(F32) for p in parts], axis=1).reshape(128, 256).T

        rest = got[own, :, TAIL : TAIL + 128].astype(F32)
        parts = [rest if u == 0 else pltpu.roll(rest, 128 - 32 * u, axis=2) for u in range(4)]
        extra = jnp.concatenate(parts, axis=1).reshape(128, 128).T
        for s in range(3):
            for n in range(3):
                at = 3 * s + n
                total = extra[at : at + 1] + extra[9 + at : 10 + at] + extra[18 + at : 19 + at]
                dshort[s, n : n + 1, cols] = total

        def back(s):
            seq = stage.at[j, s]
            tap = [w[s, n : n + 1, cols] for n in range(3)]
            total = tap[0] * seq[0:256, :] + tap[1] * seq[1:257, :] + tap[2] * seq[2:258, :]
            return total.astype(BF16)

        inner = columns(256)
        mixed[:, cols] = (query[:, cols].astype(F32) * inner).astype(BF16)
        stage[j, 0, 0:256, :] = rounded(c[:, cols].astype(F32) * inner)
        stage[j, 0, 256:258, :] = rounded(nxt[4:6, cols] * extra[29:31])
        dq[:, cols] = back(0)
        dgated = columns(0)
        stage[j, 1, 0:256, :] = dgated * cv[0:256, cols]
        stage[j, 1, 256:258, :] = extra[27:29] * cv[256:258, cols]
        dk[:, cols] = back(1)
        stage[j, 2, 0:256, :] = dgated * ck[0:256, cols]
        stage[j, 2, 256:258, :] = extra[27:29] * ck[256:258, cols]
        dv[:, cols] = back(2)


def call(kernel, outs, ins, scratch=(), flops=0, moved=0, limit=24):
    shapes, specs = [o[0] for o in outs], [o[1] for o in outs]
    one = len(outs) == 1
    return pl.pallas_call(
        kernel,
        out_shape=shapes[0] if one else shapes,
        in_specs=list(ins),
        out_specs=specs[0] if one else specs,
        scratch_shapes=list(scratch),
        compiler_params=pltpu.CompilerParams(vmem_limit_bytes=limit << 20),
        cost_estimate=pl.CostEstimate(flops=flops, bytes_accessed=moved, transcendentals=0),
    )


def shape(*dims, kind=F32):
    return jax.ShapeDtypeStruct(dims, kind)


def pack():
    packed = shape(64, 16, 512, kind=BF16)
    stream = VMEM((256, 512), BF16)
    return call(
        pack_kernel, [(packed, HBM)], [HBM] * 4,
        [stream] * 4 + [VMEM((64, 16, 512), BF16), pltpu.SemaphoreType.DMA((8,))],
        moved=2 << 20, limit=60,
    )


def channels():
    big = VMEM((128, OWN, LANES), F32)
    flat = VMEM((1024, LANES), F32)
    spectra = VMEM((OWN, 128, 256), F32)
    return call(
        channel_kernel,
        [(shape(64, 2, TAIL + 128, kind=BF16), HBM), (shape(SPARE, 128, 256), HBM), (shape(OWN, LANES), WHOLE)],
        [WHOLE] * 2 + [HBM] + [WHOLE] * 6,
        [flat, flat, flat, flat, big, VMEM((2, 128, OWN, LANES), F32), VMEM((9, 128, OWN, LANES), F32),
         VMEM((65, OWN, LANES), F32), spectra, spectra, VMEM((64, 2, TAIL + 128), BF16),
         pltpu.SemaphoreType.DMA((14,))],
        flops=4 * 10**9, moved=4 << 20, limit=50,
    )


def body(query_in, key_in, value_in, short_weights, long_filter, skip_gain, cotangent):
    t = tables()
    turns = (t["turn_re"], t["turn_im"])
    count = lax.axis_size("ctx")

    tokens = shape(256, 512, kind=BF16)
    flat = VMEM((1024, LANES), F32)
    packed = pack()(query_in, key_in, value_in, cotangent)
    seqs = lax.all_to_all(packed, "ctx", split_axis=0, concat_axis=0, tiled=True)

    here = lax.axis_index("ctx").astype(jnp.int32).reshape(1)
    spectrum = call(
        filter_kernel, [(shape(SPARE, 128, 256), WHOLE)], [WHOLE] * 5, [flat],
        flops=10**9, moved=2 << 20, limit=60,
    )(long_filter, t["first_three"], *turns, t["last"])
    own_w = call(
        weight_kernel, [(shape(10, OWN, LANES), WHOLE)],
        [pl.BlockSpec(memory_space=pltpu.SMEM), WHOLE, WHOLE, HBM], moved=1 << 20,
    )(here, short_weights, skip_gain[:, None], spectrum)

    answer, cross, dskip = channels()(
        seqs, own_w, spectrum, t["first_pair"], *turns, t["last"], t["last_back"], t["first_back"]
    )

    got = lax.all_to_all(answer, "ctx", split_axis=0, concat_axis=0, tiled=True)

    d_filter = call(
        cross_kernel, [(shape(OWN, 16384), WHOLE)], [WHOLE] * 5, [flat], flops=10**9, moved=2 << 20, limit=60
    )(cross, *turns, t["last_back"], t["first_back"])

    ends = jnp.concatenate([query_in[254:], key_in[254:], value_in[254:]], axis=0)
    starts = jnp.concatenate([key_in[:2], value_in[:2], cotangent[:2]], axis=0)
    ends, starts, _ = lax.optimization_barrier((ends, starts, d_filter))
    prev = lax.ppermute(ends, "ctx", [(i, i + 1) for i in range(count - 1)]).astype(F32)
    nxt = lax.ppermute(starts, "ctx", [(i + 1, i) for i in range(count - 1)]).astype(F32)

    extended = shape(264, 512)
    query, conv_k, conv_v = call(
        conv_kernel, [(tokens, WHOLE), (extended, WHOLE), (extended, WHOLE)], [WHOLE] * 6, moved=2 << 20
    )(query_in, key_in, value_in, prev, nxt, short_weights)
    mixed, d_query, d_key, d_value, d_short = call(
        token_kernel, [(tokens, WHOLE)] * 4 + [(shape(3, 3, 512), WHOLE)], [WHOLE] * 7,
        [VMEM((4, 3, 264, LANES), F32)], moved=3 << 20,
    )(got, query, conv_k, conv_v, cotangent, nxt, short_weights)
    return (mixed, d_query, d_key, d_value, d_filter, dskip[:, 0], d_short)


def solution(mesh):
    tokens = P("ctx", "tp")
    rows = P(("tp", "ctx"), None)
    taps = P(None, None, "tp")
    flat = P(("tp", "ctx"))
    in_specs = (tokens, tokens, tokens, taps, rows, flat, tokens)
    out_specs = (tokens, tokens, tokens, tokens, rows, flat, taps)
    return jax.shard_map(body, mesh=mesh, in_specs=in_specs, out_specs=out_specs, check_vma=False)
```
